32 devices in a mesh: seq: 16 (over z, y, x), dp: 2 (over core).
Axes of the slice: x: 2, y: 2, z: 4, core: 2. Of those that a mesh axis runs over, the one named last changes fastest.
Arguments:
- inputs: bfloat16 [2, 256, 256, 512], P('dp', 'seq'), may hold values from -6 to 6
- gate: bfloat16 [2, 256, 256, 512], P('dp', 'seq'), may hold values from -6 to 6
- kernel: bfloat16 [256, 256, 512], P(None, 'seq'), may hold values from -6 to 6
- first_blocks: bfloat16 [256, 256, 256], P('seq'), may hold values from -0.375 to 0.375
- second_blocks: bfloat16 [256, 256, 256], P('seq'), may hold values from -0.375 to 0.375
- cotangent: bfloat16 [2, 256, 256, 512], P('dp', 'seq'), may hold values from -6 to 6
Outputs:
- mixed: bfloat16 [2, 256, 256, 512], P('dp', 'seq')
- grad_inputs: bfloat16 [2, 256, 256, 512], P('dp', 'seq')
- grad_gate: bfloat16 [2, 256, 256, 512], P('dp', 'seq')
- grad_kernel: float32 [256, 256, 512], P(None, 'seq')
The draws below stay inside these ranges and needn't reach their ends.
All inputs are finite; a program needn't handle non-finite values.
Results may differ from the reference program's by a relative error of at most 0.007.
Values may be sent and summed in bfloat16 or wider, within the bound.
A program may use at most 128 MiB of HBM per device.

```python
import jax
import jax.numpy as jnp
from jax import lax

R = 256
C = 256
D = 512
SEQS = 2


def block_scale(rng, shape, pieces, low, top_value):
    def one(dim, blocks):
        draws = jax.random.uniform(jax.random.fold_in(jax.random.fold_in(rng, 6), dim), (blocks,), jnp.float32, low / len(pieces), top_value / len(pieces))
        return jnp.repeat(jnp.exp(draws), shape[dim] // blocks).reshape((-1,) + (1,) * (len(shape) - dim - 1))

    gain = one(*pieces[0])
    for cut in pieces[1:]:
        gain = gain * one(*cut)
    return gain


def normal_values(rng, shape, spread, reach, cuts=(), held_as=jnp.bfloat16):
    values = jax.random.normal(rng, shape, jnp.float32) * spread
    if len(cuts) > 0:
        values = block_scale(rng, shape, cuts, -0.22, 0.18) * values
    return jnp.clip(values, min=-reach, max=reach).astype(held_as)


def setup_inputs(seed: int = 0) -> dict:
    key_of = jax.random.split(jax.random.key(seed), 7)
    inputs = normal_values(key_of[0], (SEQS, R, C, D), 1.0, 6.0, ((0, 2), (1, 16)))
    gate = normal_values(key_of[1], (SEQS, R, C, D), 1.0, 6.0, ((0, 2), (1, 16)))
    kernel = normal_values(key_of[2], (R, C, D), 1.0, 6.0, ((1, 16),))
    first_blocks = normal_values(key_of[3], (R, C, C), C ** -0.5, 0.375, ((0, 16),))
    second_blocks = normal_values(key_of[4], (C, R, R), R ** -0.5, 0.375, ((0, 16),))
    cotangent = normal_values(key_of[5], (SEQS, R, C, D), 1.0, 6.0, ((0, 2), (1, 16)))
    return dict(inputs=inputs, gate=gate, kernel=kernel, first_blocks=first_blocks, second_blocks=second_blocks, cotangent=cotangent)


def one_sequence(inputs, gate, cotangent, kernel, first_blocks, second_blocks):
    f32 = jnp.float32
    bf16 = jnp.bfloat16
    kern = kernel.astype(f32)
    blk1 = first_blocks.astype(f32)
    blk2 = second_blocks.astype(f32)
    first = jnp.einsum('rij,rjd->rid', blk1, inputs.astype(f32)).astype(bf16)
    second = jnp.einsum('cqr,rcd->qcd', blk2, first.astype(f32))
    hidden = (second * kern).astype(bf16)
    third = jnp.einsum('cqr,qcd->rcd', blk2, hidden.astype(f32)).astype(bf16)
    result = jnp.einsum('rij,rid->rjd', blk1, third.astype(f32))
    gate32 = gate.astype(f32)
    mixed = (result * gate32).astype(bf16)
    cot = cotangent.astype(f32)
    d_result = (cot * gate32).astype(bf16)
    grad_gate = (cot * result).astype(bf16)
    d_third = jnp.einsum('rij,rjd->rid', blk1, d_result.astype(f32)).astype(bf16)
    d_hidden = jnp.einsum('cqr,rcd->qcd', blk2, d_third.astype(f32))
    grad_kernel = d_hidden * second
    d_second = (d_hidden * kern).astype(bf16)
    d_first = jnp.einsum('cqr,qcd->rcd', blk2, d_second.astype(f32)).astype(bf16)
    grad_inputs = jnp.einsum('rij,rid->rjd', blk1, d_first.astype(f32)).astype(bf16)
    return mixed, grad_inputs, grad_gate, grad_kernel


def reference(inputs, gate, kernel, first_blocks, second_blocks, cotangent):
    f32 = jnp.float32

    def step(carry, items):
        outs = one_sequence(items[0], items[1], items[2], kernel, first_blocks, second_blocks)
        return carry + outs[3], outs[:3]

    init = jnp.zeros((R, C, D), f32)
    total, stacked = lax.scan(step, init, (inputs, gate, cotangent))
    return stacked[0], stacked[1], stacked[2], total
```

```python
import functools

import jax
import jax.numpy as jnp
from jax import lax
from jax.experimental import pallas as pl
from jax.experimental.pallas import tpu as pltpu
from jax.sharding import PartitionSpec as P

MESH = pl.DeviceIdType.MESH
LANES = 128
EARLY = 2


def fused(
    n,
    x_hbm,
    gate_hbm,
    kern_hbm,
    a_hbm,
    b_hbm,
    cot_hbm,
    mixed_hbm,
    gin_hbm,
    ggate_hbm,
    gk_hbm,
    part_hbm,
    a,
    b,
    x,
    gate,
    cot,
    send_f,
    send_b,
    recv_1f,
    recv_1b,
    recv_2f,
    recv_2b,
    second,
    turn,
    kst,
    tmp,
    load_sem,
    tmp_sem,
    out_sem,
    row_sem,
    send_sem,
    recv_sem,
    dp_send,
    dp_recv,
):
    f32 = jnp.float32
    bf16 = jnp.bfloat16
    own, cols, width = x.shape
    rows = cols
    half = n // 2
    cut = cols // 2
    slabs = width // LANES
    block = own * own
    me = lax.axis_index("seq")
    other = 1 - lax.axis_index("dp")
    near_half = me // half
    far_half = 1 - near_half
    spot = me % half

    def load(src, dst, i):
        return pltpu.make_async_copy(src, dst, load_sem.at[i])

    load(a_hbm, a, 0).start()
    load(x_hbm, x, 1).start()
    load(gate_hbm, gate, 2).start()
    load(cot_hbm, cot, 3).start()
    load(b_hbm, b, 4).start()

    barrier = pltpu.get_barrier_semaphore()

    @pl.loop(1, n)
    def _(i):
        pl.semaphore_signal(
            barrier, inc=1, device_id={"seq": (me + i) % n}, device_id_type=MESH
        )

    pl.semaphore_signal(barrier, inc=1, device_id={"dp": other}, device_id_type=MESH)
    pl.semaphore_wait(barrier, n)

    def lane(k):
        return pl.ds(k * LANES, LANES)

    def message(stage, send, recv, to, slot):
        return pltpu.make_async_remote_copy(
            src_ref=send.at[to],
            dst_ref=recv.at[slot],
            send_sem=send_sem.at[stage, to],
            recv_sem=recv_sem.at[stage, slot],
            device_id={"seq": to},
            device_id_type=MESH,
        )

    def wait_sent(stage, send, recv):
        @pl.loop(1, n)
        def _(i):
            to = (me + i) % n
            message(stage, send, recv, to, to).wait_send()

    def wait_arrived(stage, send, recv):
        @pl.loop(1, n)
        def _(i):
            slot = (me + i) % n
            message(stage, send, recv, slot, slot).wait_recv()

    def produce(side, product, send):
        at = pl.multiple_of(side * cut, cut)

        @pl.loop(0, own)
        def _(e):
            value = product(e, at)
            for k in range(slabs):
                turn[k, pl.ds(e, cut, stride=own), :] = value[
                    :, k * LANES : (k + 1) * LANES
                ]

        @pl.loop(0, half)
        def _(j):
            for k in range(slabs):
                piece = turn[k, pl.ds(pl.multiple_of(j * block, block), block), :]
                send[side * half + j, :, :, k * LANES : (k + 1) * LANES] = piece.reshape(
                    own, own, LANES
                ).astype(bf16)

    def exchange(stage, product, send, recv):
        def to_far(j):
            to = far_half * half + (spot + j) % half
            message(stage, send, recv, to, me).start()

        def to_near(j):
            to = near_half * half + (spot + 1 + j) % half
            message(stage, send, recv, to, me).start()

        produce(far_half, product, send)

        @pl.loop(0, EARLY)
        def _(j):
            to_far(j)

        produce(near_half, product, send)

        @pl.loop(0, half - 1)
        def _(j):
            to_near(j)

            @pl.when(j < half - EARLY)
            def _():
                to_far(j + EARLY)

        recv[me] = send[me]

    def spread(e, at):
        return jnp.dot(a[e, pl.ds(at, cut), :], x[e], preferred_element_type=f32)

    def unmix(held):
        def product(e, at):
            values = held[:, e].reshape(rows, width)
            return lax.dot_general(
                b[e, :, pl.ds(at, cut)],
                values,
                (((0,), (0,)), ((), ())),
                preferred_element_type=f32,
            )

        return product

    def finish(held, e):
        return lax.dot_general(
            a[e],
            held[:, e].reshape(cols, width),
            (((0,), (0,)), ((), ())),
            preferred_element_type=f32,
        )

    load(a_hbm, a, 0).wait()
    load(x_hbm, x, 1).wait()
    exchange(0, spread, send_f, recv_1f)

    load(gate_hbm, gate, 2).wait()
    load(cot_hbm, cot, 3).wait()

    @pl.loop(0, own)
    def _(e):
        x[e] = (cot[e].astype(f32) * gate[e].astype(f32)).astype(bf16)

    exchange(1, spread, send_b, recv_1b)

    quarter = kst.shape[0] // own

    @pl.loop(0, rows // quarter)
    def _(i):
        size = quarter * own
        take = load(kern_hbm.at[pl.ds(pl.multiple_of(i * size, size), size), :], kst, 1)
        take.start()
        take.wait()
        for k in range(slabs):
            turn[k, 0:size, :] = kst[:, k * LANES : (k + 1) * LANES].astype(f32)

        @pl.loop(0, own)
        def _(e):
            for k in range(slabs):
                x[
                    e,
                    pl.ds(pl.multiple_of(i * quarter, quarter), quarter),
                    k * LANES : (k + 1) * LANES,
                ] = turn[k, pl.ds(e, quarter, stride=own), :].astype(bf16)

    load(b_hbm, b, 4).wait()
    wait_arrived(0, send_f, recv_1f)

    @pl.loop(0, own)
    def _(e):
        value = jnp.dot(
            b[e], recv_1f[:, e].reshape(rows, width), preferred_element_type=f32
        )
        second[e] = value
        recv_1f[:, e] = (value * x[e].astype(f32)).astype(bf16).reshape(n, own, width)

    wait_sent(0, send_f, recv_1f)
    exchange(2, unmix(recv_1f), send_f, recv_2f)

    wait_arrived(1, send_b, recv_1b)

    @pl.loop(0, own)
    def _(e):
        value = jnp.dot(
            b[e], recv_1b[:, e].reshape(rows, width), preferred_element_type=f32
        )
        second[e] = second[e] * value
        recv_1b[:, e] = (value * x[e].astype(f32)).astype(bf16).reshape(n, own, width)

    swap = pltpu.make_async_remote_copy(
        src_ref=second,
        dst_ref=part_hbm,
        send_sem=dp_send,
        recv_sem=dp_recv,
        device_id={"dp": other},
        device_id_type=MESH,
    )
    swap.start()
    wait_sent(1, send_b, recv_1b)
    exchange(3, unmix(recv_1b), send_b, recv_2b)

    swap.wait_recv()
    for side in range(2):
        at = side * cut

        def part(e, slot):
            return pltpu.make_async_copy(
                part_hbm.at[e, pl.ds(at, cut), :], tmp.at[slot], tmp_sem.at[slot]
            )

        part(0, 0).start()

        @pl.loop(0, own)
        def _(e):
            @pl.when(e < own - 1)
            def _():
                part(e + 1, (e + 1) % 2).start()

            part(e, e % 2).wait()
            total = second[e, at : at + cut, :] + tmp[e % 2]
            for k in range(slabs):
                turn[k, pl.ds(e, cut, stride=own), :] = total[
                    :, k * LANES : (k + 1) * LANES
                ]

        outs = [
            pltpu.make_async_copy(
                turn.at[k],
                gk_hbm.at[pl.ds(at * own, cut * own), lane(k)],
                out_sem.at[k],
            )
            for k in range(slabs)
        ]
        for out in outs:
            out.start()
        for out in outs:
            out.wait()

    wait_arrived(2, send_f, recv_2f)

    @pl.loop(0, own)
    def _(e):
        result = finish(recv_2f, e)
        mixed = (result * gate[e].astype(f32)).astype(bf16)
        ggate = (cot[e].astype(f32) * result).astype(bf16)
        gate[e] = mixed
        cot[e] = ggate

    out_mixed = load(gate, mixed_hbm, 2)
    out_ggate = load(cot, ggate_hbm, 3)
    out_mixed.start()
    out_ggate.start()

    swap.wait_send()
    wait_sent(2, send_f, recv_2f)
    wait_arrived(3, send_b, recv_2b)

    def out_row(e):
        return pltpu.make_async_copy(x.at[e], gin_hbm.at[e], row_sem.at[e])

    @pl.loop(0, own)
    def _(e):
        x[e] = finish(recv_2b, e).astype(bf16)
        out_row(e).start()

    wait_sent(3, send_b, recv_2b)
    out_mixed.wait()
    out_ggate.wait()

    @pl.loop(0, own)
    def _(e):
        out_row(e).wait()


def fused_shards(n, inputs, gate, kernel, first_blocks, second_blocks, cotangent):
    f32 = jnp.float32
    bf16 = jnp.bfloat16
    _, own, cols, width = inputs.shape
    rows = kernel.shape[0]
    slabs = width // LANES
    here = jax.ShapeDtypeStruct((own, cols, width), bf16)
    anywhere = pl.BlockSpec(memory_space=pl.ANY)
    wire = pltpu.VMEM((n, own, own, width), bf16)
    held = pltpu.VMEM((own, cols, width), bf16)
    dma = pltpu.SemaphoreType.DMA
    mixed, gin, ggate, gk, _ = pl.pallas_call(
        functools.partial(fused, n),
        out_shape=(
            here,
            here,
            here,
            jax.ShapeDtypeStruct((rows * own, width), f32),
            jax.ShapeDtypeStruct((own, rows, width), f32),
        ),
        in_specs=[anywhere] * 6,
        out_specs=[anywhere] * 5,
        scratch_shapes=[
            pltpu.VMEM((own, cols, cols), bf16),
            pltpu.VMEM((own, rows, rows), bf16),
            held,
            held,
            held,
            wire,
            wire,
            wire,
            wire,
            wire,
            wire,
            pltpu.VMEM((own, rows, width), f32),
            pltpu.VMEM((slabs, cols // 2 * own, LANES), f32),
            pltpu.VMEM((rows // 4 * own, width), bf16),
            pltpu.VMEM((2, rows // 2, width), f32),
            dma((5,)),
            dma((2,)),
            dma((slabs,)),
            dma((own,)),
            dma((4, n)),
            dma((4, n)),
            dma,
            dma,
        ],
        compiler_params=pltpu.CompilerParams(
            collective_id=0, has_side_effects=True, vmem_limit_bytes=60 << 20
        ),
        cost_estimate=pl.CostEstimate(
            flops=16 * own * cols * cols * width,
            bytes_accessed=48 * own * cols * width,
            transcendentals=0,
        ),
    )(
        inputs.reshape(own, cols, width),
        gate.reshape(own, cols, width),
        kernel.reshape(rows * own, width),
        first_blocks,
        second_blocks,
        cotangent.reshape(own, cols, width),
    )
    shape = inputs.shape
    return (
        mixed.reshape(shape),
        gin.reshape(shape),
        ggate.reshape(shape),
        gk.reshape(rows, own, width),
    )


def shards(inputs, gate, kernel, first_blocks, second_blocks, cotangent):
    f32 = jnp.float32
    bf16 = jnp.bfloat16
    gate32 = gate.astype(f32)
    cot = cotangent.astype(f32)
    d_result = (cot * gate32).astype(bf16)

    def spread(rows):
        return jnp.einsum("rij,srjd->srid", first_blocks, rows, preferred_element_type=f32).astype(
            bf16
        )

    def mix_columns(piece):
        return jnp.einsum("cqr,srcd->sqcd", second_blocks, piece, preferred_element_type=f32)

    def unmix_columns(scaled):
        return jnp.einsum(
            "cqr,sqcd->srcd", second_blocks, scaled, preferred_element_type=f32
        ).astype(bf16)

    def finish_rows(piece):
        return jnp.einsum("rij,srid->srjd", first_blocks, piece, preferred_element_type=f32)

    second = mix_columns(
        lax.all_to_all(spread(inputs), "seq", split_axis=2, concat_axis=1, tiled=True)
    )
    hidden = (second * kernel).astype(bf16)
    result = finish_rows(
        lax.all_to_all(unmix_columns(hidden), "seq", split_axis=1, concat_axis=2, tiled=True)
    )
    d_hidden = mix_columns(
        lax.all_to_all(spread(d_result), "seq", split_axis=2, concat_axis=1, tiled=True)
    )
    d_second = (d_hidden * kernel).astype(bf16)
    d_inputs = finish_rows(
        lax.all_to_all(unmix_columns(d_second), "seq", split_axis=1, concat_axis=2, tiled=True)
    )
    mixed = (result * gate32).astype(bf16)
    grad_gate = (cot * result).astype(bf16)
    grad_inputs = d_inputs.astype(bf16)
    grad_kernel = lax.psum(jnp.sum(d_hidden * second, axis=0), "dp")
    return (mixed, grad_inputs, grad_gate, grad_kernel)


def solution(mesh):
    placed = (
        P("dp", "seq", None, None),
        P("dp", "seq", None, None),
        P(None, "seq", None),
        P("seq", None, None),
        P("seq", None, None),
        P("dp", "seq", None, None),
    )
    def program(inputs, gate, kernel, first_blocks, second_blocks, cotangent):
        n = mesh.shape["seq"]
        seqs, rows, cols, width = inputs.shape
        fits = (
            mesh.shape["dp"] == 2
            and seqs == 2
            and rows == cols
            and n % 2 == 0
            and rows % (16 * n) == 0
            and rows % 256 == 0
            and width % LANES == 0
        )
        body = functools.partial(fused_shards, n) if fits else shards
        return placed_body(body)(
            inputs, gate, kernel, first_blocks, second_blocks, cotangent
        )

    def placed_body(body):
        return jax.shard_map(
            body,
            mesh=mesh,
            in_specs=placed,
            out_specs=(
                P("dp", "seq", None, None),
                P("dp", "seq", None, None),
                P("dp", "seq", None, None),
                P(None, "seq", None),
            ),
            check_vma=False,
        )

    return program
```

```python
import functools

import jax
import jax.numpy as jnp
from jax import lax
from jax.experimental import pallas as pl
from jax.experimental.pallas import tpu as pltpu
from jax.sharding import PartitionSpec as P

MESH = pl.DeviceIdType.MESH
LANES = 128
LAG = 2


def fused(
    n,
    x_hbm,
    gate_hbm,
    kern_hbm,
    a_hbm,
    b_hbm,
    cot_hbm,
    mixed_hbm,
    gin_hbm,
    ggate_hbm,
    gk_hbm,
    part_hbm,
    a,
    b,
    x,
    gate,
    cot,
    send_f,
    send_b,
    recv_1f,
    recv_1b,
    recv_2f,
    recv_2b,
    second,
    turn,
    kst,
    tmp,
    load_sem,
    tmp_sem,
    out_sem,
    row_sem,
    send_sem,
    recv_sem,
    dp_send,
    dp_recv,
):
    f32 = jnp.float32
    bf16 = jnp.bfloat16
    own, cols, width = x.shape
    rows = cols
    half = n // 2
    cut = cols // 2
    slabs = width // LANES
    block = own * own
    me = lax.axis_index("seq")
    other = 1 - lax.axis_index("dp")
    near_half = me // half
    far_half = 1 - near_half
    spot = me % half

    def load(src, dst, i):
        return pltpu.make_async_copy(src, dst, load_sem.at[i])

    load(a_hbm, a, 0).start()
    load(x_hbm, x, 1).start()
    load(gate_hbm, gate, 2).start()
    load(cot_hbm, cot, 3).start()
    load(b_hbm, b, 4).start()

    barrier = pltpu.get_barrier_semaphore()

    @pl.loop(1, n)
    def _(i):
        pl.semaphore_signal(
            barrier, inc=1, device_id={"seq": (me + i) % n}, device_id_type=MESH
        )

    pl.semaphore_signal(barrier, inc=1, device_id={"dp": other}, device_id_type=MESH)
    pl.semaphore_wait(barrier, n)

    def lane(k):
        return pl.ds(k * LANES, LANES)

    def message(stage, send, recv, to, slot):
        return pltpu.make_async_remote_copy(
            src_ref=send.at[to],
            dst_ref=recv.at[slot],
            send_sem=send_sem.at[stage, to],
            recv_sem=recv_sem.at[stage, slot],
            device_id={"seq": to},
            device_id_type=MESH,
        )

    def wait_sent(stage, send, recv):
        @pl.loop(1, n)
        def _(i):
            to = (me + i) % n
            message(stage, send, recv, to, to).wait_send()

    def wait_arrived(stage, send, recv):
        @pl.loop(1, n)
        def _(i):
            slot = (me + i) % n
            message(stage, send, recv, slot, slot).wait_recv()

    def produce(side, product, send):
        at = pl.multiple_of(side * cut, cut)

        @pl.loop(0, own)
        def _(e):
            value = product(e, at)
            for k in range(slabs):
                turn[k, pl.ds(e, cut, stride=own), :] = value[
                    :, k * LANES : (k + 1) * LANES
                ]

        @pl.loop(0, half)
        def _(j):
            for k in range(slabs):
                piece = turn[k, pl.ds(pl.multiple_of(j * block, block), block), :]
                send[side * half + j, :, :, k * LANES : (k + 1) * LANES] = piece.reshape(
                    own, own, LANES
                ).astype(bf16)

    def order(i):
        far = 1 - i % 2
        side = far * far_half + (1 - far) * near_half
        return side * half + (spot + (1 - far) + i // 2) % half

    def start(stage, send, recv, i):
        message(stage, send, recv, order(i), me).start()

    def left(stage, send, recv, i):
        to = order(i)
        message(stage, send, recv, to, to).wait_send()

    def produce_all(product, send, recv):
        produce(far_half, product, send)
        produce(near_half, product, send)
        recv[me] = send[me]

    def issue(stage, send, recv, before):
        @pl.loop(0, n - 1)
        def _(i):
            @pl.when(i >= LAG)
            def _():
                left(*before, i - LAG)

            start(stage, send, recv, i)

        @pl.loop(n - 1 - LAG, n - 1)
        def _(i):
            left(*before, i)

    def spread(e, at):
        return jnp.dot(a[e, pl.ds(at, cut), :], x[e], preferred_element_type=f32)

    def unmix(held):
        def product(e, at):
            values = held[:, e].reshape(rows, width)
            return lax.dot_general(
                b[e, :, pl.ds(at, cut)],
                values,
                (((0,), (0,)), ((), ())),
                preferred_element_type=f32,
            )

        return product

    def finish(held, e):
        return lax.dot_general(
            a[e],
            held[:, e].reshape(cols, width),
            (((0,), (0,)), ((), ())),
            preferred_element_type=f32,
        )

    load(a_hbm, a, 0).wait()
    load(x_hbm, x, 1).wait()
    produce(far_half, spread, send_f)
    start(0, send_f, recv_1f, 0)
    start(0, send_f, recv_1f, 2)
    produce(near_half, spread, send_f)
    start(0, send_f, recv_1f, 1)

    @pl.loop(3, n - 1)
    def _(i):
        start(0, send_f, recv_1f, i)

    recv_1f[me] = send_f[me]

    load(gate_hbm, gate, 2).wait()
    load(cot_hbm, cot, 3).wait()

    @pl.loop(0, own)
    def _(e):
        x[e] = (cot[e].astype(f32) * gate[e].astype(f32)).astype(bf16)

    produce_all(spread, send_b, recv_1b)

    quarter = kst.shape[0] // own

    @pl.loop(0, rows // quarter)
    def _(i):
        size = quarter * own
        take = load(kern_hbm.at[pl.ds(pl.multiple_of(i * size, size), size), :], kst, 1)
        take.start()
        take.wait()
        for k in range(slabs):
            turn[k, 0:size, :] = kst[:, k * LANES : (k + 1) * LANES].astype(f32)

        @pl.loop(0, own)
        def _(e):
            for k in range(slabs):
                x[
                    e,
                    pl.ds(pl.multiple_of(i * quarter, quarter), quarter),
                    k * LANES : (k + 1) * LANES,
                ] = turn[k, pl.ds(e, quarter, stride=own), :].astype(bf16)

    issue(1, send_b, recv_1b, (0, send_f, recv_1f))

    load(b_hbm, b, 4).wait()
    wait_arrived(0, send_f, recv_1f)

    @pl.loop(0, own)
    def _(e):
        value = jnp.dot(
            b[e], recv_1f[:, e].reshape(rows, width), preferred_element_type=f32
        )
        second[e] = value
        recv_1f[:, e] = (value * x[e].astype(f32)).astype(bf16).reshape(n, own, width)

    produce_all(unmix(recv_1f), send_f, recv_2f)
    issue(2, send_f, recv_2f, (1, send_b, recv_1b))

    wait_arrived(1, send_b, recv_1b)

    @pl.loop(0, own)
    def _(e):
        value = jnp.dot(
            b[e], recv_1b[:, e].reshape(rows, width), preferred_element_type=f32
        )
        second[e] = second[e] * value
        recv_1b[:, e] = (value * x[e].astype(f32)).astype(bf16).reshape(n, own, width)

    swap = pltpu.make_async_remote_copy(
        src_ref=second,
        dst_ref=part_hbm,
        send_sem=dp_send,
        recv_sem=dp_recv,
        device_id={"dp": other},
        device_id_type=MESH,
    )
    swap.start()
    produce_all(unmix(recv_1b), send_b, recv_2b)

    swap.wait_recv()
    for side in range(2):
        at = side * cut

        def part(e, slot):
            return pltpu.make_async_copy(
                part_hbm.at[e, pl.ds(at, cut), :], tmp.at[slot], tmp_sem.at[slot]
            )

        part(0, 0).start()

        @pl.loop(0, own)
        def _(e):
            @pl.when(e < own - 1)
            def _():
                part(e + 1, (e + 1) % 2).start()

            part(e, e % 2).wait()
            total = second[e, at : at + cut, :] + tmp[e % 2]
            for k in range(slabs):
                turn[k, pl.ds(e, cut, stride=own), :] = total[
                    :, k * LANES : (k + 1) * LANES
                ]

        outs = [
            pltpu.make_async_copy(
                turn.at[k],
                gk_hbm.at[pl.ds(at * own, cut * own), lane(k)],
                out_sem.at[k],
            )
            for k in range(slabs)
        ]
        for out in outs:
            out.start()
        for out in outs:
            out.wait()

    issue(3, send_b, recv_2b, (2, send_f, recv_2f))

    wait_arrived(2, send_f, recv_2f)

    @pl.loop(0, own)
    def _(e):
        result = finish(recv_2f, e)
        mixed = (result * gate[e].astype(f32)).astype(bf16)
        ggate = (cot[e].astype(f32) * result).astype(bf16)
        gate[e] = mixed
        cot[e] = ggate

    out_mixed = load(gate, mixed_hbm, 2)
    out_ggate = load(cot, ggate_hbm, 3)
    out_mixed.start()
    out_ggate.start()

    swap.wait_send()
    wait_arrived(3, send_b, recv_2b)

    def out_row(e):
        return pltpu.make_async_copy(x.at[e], gin_hbm.at[e], row_sem.at[e])

    @pl.loop(0, own)
    def _(e):
        x[e] = finish(recv_2b, e).astype(bf16)
        out_row(e).start()

    wait_sent(3, send_b, recv_2b)
    out_mixed.wait()
    out_ggate.wait()

    @pl.loop(0, own)
    def _(e):
        out_row(e).wait()


def fused_shards(n, inputs, gate, kernel, first_blocks, second_blocks, cotangent):
    f32 = jnp.float32
    bf16 = jnp.bfloat16
    _, own, cols, width = inputs.shape
    rows = kernel.shape[0]
    slabs = width // LANES
    here = jax.ShapeDtypeStruct((own, cols, width), bf16)
    anywhere = pl.BlockSpec(memory_space=pl.ANY)
    wire = pltpu.VMEM((n, own, own, width), bf16)
    held = pltpu.VMEM((own, cols, width), bf16)
    dma = pltpu.SemaphoreType.DMA
    mixed, gin, ggate, gk, _ = pl.pallas_call(
        functools.partial(fused, n),
        out_shape=(
            here,
            here,
            here,
            jax.ShapeDtypeStruct((rows * own, width), f32),
            jax.ShapeDtypeStruct((own, rows, width), f32),
        ),
        in_specs=[anywhere] * 6,
        out_specs=[anywhere] * 5,
        scratch_shapes=[
            pltpu.VMEM((own, cols, cols), bf16),
            pltpu.VMEM((own, rows, rows), bf16),
            held,
            held,
            held,
            wire,
            wire,
            wire,
            wire,
            wire,
            wire,
            pltpu.VMEM((own, rows, width), f32),
            pltpu.VMEM((slabs, cols // 2 * own, LANES), f32),
            pltpu.VMEM((rows // 4 * own, width), bf16),
            pltpu.VMEM((2, rows // 2, width), f32),
            dma((5,)),
            dma((2,)),
            dma((slabs,)),
            dma((own,)),
            dma((4, n)),
            dma((4, n)),
            dma,
            dma,
        ],
        compiler_params=pltpu.CompilerParams(
            collective_id=0, has_side_effects=True, vmem_limit_bytes=60 << 20
        ),
        cost_estimate=pl.CostEstimate(
            flops=16 * own * cols * cols * width,
            bytes_accessed=48 * own * cols * width,
            transcendentals=0,
        ),
    )(
        inputs.reshape(own, cols, width),
        gate.reshape(own, cols, width),
        kernel.reshape(rows * own, width),
        first_blocks,
        second_blocks,
        cotangent.reshape(own, cols, width),
    )
    shape = inputs.shape
    return (
        mixed.reshape(shape),
        gin.reshape(shape),
        ggate.reshape(shape),
        gk.reshape(rows, own, width),
    )


def shards(inputs, gate, kernel, first_blocks, second_blocks, cotangent):
    f32 = jnp.float32
    bf16 = jnp.bfloat16
    gate32 = gate.astype(f32)
    cot = cotangent.astype(f32)
    d_result = (cot * gate32).astype(bf16)

    def spread(rows):
        return jnp.einsum("rij,srjd->srid", first_blocks, rows, preferred_element_type=f32).astype(
            bf16
        )

    def mix_columns(piece):
        return jnp.einsum("cqr,srcd->sqcd", second_blocks, piece, preferred_element_type=f32)

    def unmix_columns(scaled):
        return jnp.einsum(
            "cqr,sqcd->srcd", second_blocks, scaled, preferred_element_type=f32
        ).astype(bf16)

    def finish_rows(piece):
        return jnp.einsum("rij,srid->srjd", first_blocks, piece, preferred_element_type=f32)

    second = mix_columns(
        lax.all_to_all(spread(inputs), "seq", split_axis=2, concat_axis=1, tiled=True)
    )
    hidden = (second * kernel).astype(bf16)
    result = finish_rows(
        lax.all_to_all(unmix_columns(hidden), "seq", split_axis=1, concat_axis=2, tiled=True)
    )
    d_hidden = mix_columns(
        lax.all_to_all(spread(d_result), "seq", split_axis=2, concat_axis=1, tiled=True)
    )
    d_second = (d_hidden * kernel).astype(bf16)
    d_inputs = finish_rows(
        lax.all_to_all(unmix_columns(d_second), "seq", split_axis=1, concat_axis=2, tiled=True)
    )
    mixed = (result * gate32).astype(bf16)
    grad_gate = (cot * result).astype(bf16)
    grad_inputs = d_inputs.astype(bf16)
    grad_kernel = lax.psum(jnp.sum(d_hidden * second, axis=0), "dp")
    return (mixed, grad_inputs, grad_gate, grad_kernel)


def solution(mesh):
    placed = (
        P("dp", "seq", None, None),
        P("dp", "seq", None, None),
        P(None, "seq", None),
        P("seq", None, None),
        P("seq", None, None),
        P("dp", "seq", None, None),
    )
    def program(inputs, gate, kernel, first_blocks, second_blocks, cotangent):
        n = mesh.shape["seq"]
        seqs, rows, cols, width = inputs.shape
        fits = (
            mesh.shape["dp"] == 2
            and seqs == 2
            and rows == cols
            and n % 2 == 0
            and rows % (16 * n) == 0
            and rows % 256 == 0
            and width % LANES == 0
        )
        body = functools.partial(fused_shards, n) if fits else shards
        return placed_body(body)(
            inputs, gate, kernel, first_blocks, second_blocks, cotangent
        )

    def placed_body(body):
        return jax.shard_map(
            body,
            mesh=mesh,
            in_specs=placed,
            out_specs=(
                P("dp", "seq", None, None),
                P("dp", "seq", None, None),
                P("dp", "seq", None, None),
                P(None, "seq", None),
            ),
            check_vma=False,
        )

    return program
```

```python
import functools

import jax
import jax.numpy as jnp
from jax import lax
from jax.experimental import pallas as pl
from jax.experimental.pallas import tpu as pltpu
from jax.sharding import PartitionSpec as P

MESH = pl.DeviceIdType.MESH
LANES = 128
LAG = 2
PIECES = 4


def fused(
    n,
    x_hbm,
    gate_hbm,
    kern_hbm,
    a_hbm,
    b_hbm,
    cot_hbm,
    mixed_hbm,
    recv_2b,
    ggate_hbm,
    gk_hbm,
    part_hbm,
    a,
    b,
    x,
    gate,
    cot,
    send_f,
    send_b,
    recv_1f,
    recv_1b,
    recv_2f,
    second,
    turn,
    kst,
    tmp,
    load_sem,
    tmp_sem,
    out_sem,
    send_sem,
    recv_sem,
    dp_send,
    dp_recv,
):
    f32 = jnp.float32
    bf16 = jnp.bfloat16
    own, cols, width = x.shape
    rows = cols
    half = n // 2
    cut = cols // 2
    slabs = width // LANES
    block = own * own
    me = lax.axis_index("seq")
    other = 1 - lax.axis_index("dp")
    near_half = me // half
    far_half = 1 - near_half
    spot = me % half

    def load(src, dst, i):
        return pltpu.make_async_copy(src, dst, load_sem.at[i])

    load(a_hbm, a, 0).start()
    load(x_hbm, x, 1).start()
    load(gate_hbm, gate, 2).start()
    load(cot_hbm, cot, 3).start()
    load(b_hbm, b, 4).start()

    barrier = pltpu.get_barrier_semaphore()

    @pl.loop(1, n)
    def _(i):
        pl.semaphore_signal(
            barrier, inc=1, device_id={"seq": (me + i) % n}, device_id_type=MESH
        )

    pl.semaphore_signal(barrier, inc=1, device_id={"dp": other}, device_id_type=MESH)
    pl.semaphore_wait(barrier, n)

    def lane(k):
        return pl.ds(k * LANES, LANES)

    def message(stage, send, recv, to, slot):
        return pltpu.make_async_remote_copy(
            src_ref=send.at[to],
            dst_ref=recv.at[slot],
            send_sem=send_sem.at[stage, to],
            recv_sem=recv_sem.at[stage, slot],
            device_id={"seq": to},
            device_id_type=MESH,
        )

    def wait_sent(stage, send, recv):
        @pl.loop(1, n)
        def _(i):
            to = (me + i) % n
            message(stage, send, recv, to, to).wait_send()

    def wait_arrived(stage, send, recv):
        @pl.loop(1, n)
        def _(i):
            slot = (me + i) % n
            message(stage, send, recv, slot, slot).wait_recv()

    def produce(side, product, send):
        at = pl.multiple_of(side * cut, cut)

        @pl.loop(0, own)
        def _(e):
            value = product(e, at)
            for k in range(slabs):
                turn[k, pl.ds(e, cut, stride=own), :] = value[
                    :, k * LANES : (k + 1) * LANES
                ]

        @pl.loop(0, half)
        def _(j):
            for k in range(slabs):
                piece = turn[k, pl.ds(pl.multiple_of(j * block, block), block), :]
                send[side * half + j, :, :, k * LANES : (k + 1) * LANES] = piece.reshape(
                    own, own, LANES
                ).astype(bf16)

    def order(i):
        far = 1 - i % 2
        side = far * far_half + (1 - far) * near_half
        return side * half + (spot + (1 - far) + i // 2) % half

    def start(stage, send, recv, i):
        message(stage, send, recv, order(i), me).start()

    def left(stage, send, recv, i):
        to = order(i)
        message(stage, send, recv, to, to).wait_send()

    def produce_all(product, send):
        produce(far_half, product, send)
        produce(near_half, product, send)

    def issue(stage, send, recv, before):
        @pl.loop(0, n - 1)
        def _(i):
            @pl.when(i >= LAG)
            def _():
                left(*before, i - LAG)

            start(stage, send, recv, i)

        @pl.loop(n - 1 - LAG, n - 1)
        def _(i):
            left(*before, i)

    def spread(e, at):
        return jnp.dot(a[e, pl.ds(at, cut), :], x[e], preferred_element_type=f32)

    def unmix(held):
        def product(e, at):
            values = held[:, e].reshape(rows, width)
            return lax.dot_general(
                b[e, :, pl.ds(at, cut)],
                values,
                (((0,), (0,)), ((), ())),
                preferred_element_type=f32,
            )

        return product

    def finish(held, e):
        return lax.dot_general(
            a[e],
            held[:, e].reshape(cols, width),
            (((0,), (0,)), ((), ())),
            preferred_element_type=f32,
        )

    load(a_hbm, a, 0).wait()
    load(x_hbm, x, 1).wait()
    produce(far_half, spread, send_f)
    start(0, send_f, recv_1f, 0)
    start(0, send_f, recv_1f, 2)
    produce(near_half, spread, send_f)
    start(0, send_f, recv_1f, 1)

    @pl.loop(3, n - 1)
    def _(i):
        start(0, send_f, recv_1f, i)

    recv_1f[me] = send_f[me]

    load(gate_hbm, gate, 2).wait()
    load(cot_hbm, cot, 3).wait()

    @pl.loop(0, own)
    def _(e):
        x[e] = (cot[e].astype(f32) * gate[e].astype(f32)).astype(bf16)

    produce_all(spread, send_b)
    recv_1b[me] = send_b[me]

    quarter = kst.shape[0] // own

    @pl.loop(0, rows // quarter)
    def _(i):
        size = quarter * own
        take = load(kern_hbm.at[pl.ds(pl.multiple_of(i * size, size), size), :], kst, 1)
        take.start()
        take.wait()
        for k in range(slabs):
            turn[k, 0:size, :] = kst[:, k * LANES : (k + 1) * LANES].astype(f32)

        @pl.loop(0, own)
        def _(e):
            for k in range(slabs):
                x[
                    e,
                    pl.ds(pl.multiple_of(i * quarter, quarter), quarter),
                    k * LANES : (k + 1) * LANES,
                ] = turn[k, pl.ds(e, quarter, stride=own), :].astype(bf16)

    issue(1, send_b, recv_1b, (0, send_f, recv_1f))

    load(b_hbm, b, 4).wait()
    wait_arrived(0, send_f, recv_1f)

    @pl.loop(0, own)
    def _(e):
        value = jnp.dot(
            b[e], recv_1f[:, e].reshape(rows, width), preferred_element_type=f32
        )
        second[e] = value
        recv_1f[:, e] = (value * x[e].astype(f32)).astype(bf16).reshape(n, own, width)

    produce_all(unmix(recv_1f), send_f)
    issue(2, send_f, recv_2f, (1, send_b, recv_1b))

    recv_2f[me] = send_f[me]

    wait_arrived(1, send_b, recv_1b)

    @pl.loop(0, own)
    def _(e):
        value = jnp.dot(
            b[e], recv_1b[:, e].reshape(rows, width), preferred_element_type=f32
        )
        second[e] = second[e] * value
        recv_1b[:, e] = (value * x[e].astype(f32)).astype(bf16).reshape(n, own, width)

    swap = pltpu.make_async_remote_copy(
        src_ref=second,
        dst_ref=part_hbm,
        send_sem=dp_send,
        recv_sem=dp_recv,
        device_id={"dp": other},
        device_id_type=MESH,
    )
    swap.start()
    produce_all(unmix(recv_1b), send_b)
    keep = load(send_b.at[me], recv_2b.at[me], 0)
    keep.start()

    swap.wait_recv()
    for side in range(2):
        at = side * cut

        def part(e, slot):
            return pltpu.make_async_copy(
                part_hbm.at[e, pl.ds(at, cut), :], tmp.at[slot], tmp_sem.at[slot]
            )

        part(0, 0).start()

        @pl.loop(0, own)
        def _(e):
            @pl.when(e < own - 1)
            def _():
                part(e + 1, (e + 1) % 2).start()

            part(e, e % 2).wait()
            total = second[e, at : at + cut, :] + tmp[e % 2]
            for k in range(slabs):
                turn[k, pl.ds(e, cut, stride=own), :] = total[
                    :, k * LANES : (k + 1) * LANES
                ]

        outs = [
            pltpu.make_async_copy(
                turn.at[k],
                gk_hbm.at[pl.ds(at * own, cut * own), lane(k)],
                out_sem.at[k],
            )
            for k in range(slabs)
        ]
        for out in outs:
            out.start()
        for out in outs:
            out.wait()

    issue(3, send_b, recv_2b, (2, send_f, recv_2f))

    wait_arrived(2, send_f, recv_2f)

    @pl.loop(0, own)
    def _(e):
        result = finish(recv_2f, e)
        mixed = (result * gate[e].astype(f32)).astype(bf16)
        ggate = (cot[e].astype(f32) * result).astype(bf16)
        gate[e] = mixed
        cot[e] = ggate

    out_mixed = load(gate, mixed_hbm, 2)
    out_ggate = load(cot, ggate_hbm, 3)
    out_mixed.start()
    out_ggate.start()

    swap.wait_send()
    wait_arrived(3, send_b, recv_2b)

    wait_sent(3, send_b, recv_2b)
    keep.wait()
    out_mixed.wait()
    out_ggate.wait()


def last_rows(
    a_hbm,
    held_hbm,
    mixed_in,
    ggate_in,
    gk_in,
    gin_hbm,
    mixed_out,
    ggate_out,
    gk_out,
    a,
    held,
    rows,
    in_sem,
    row_sem,
    out_sem,
):
    sources, targets = (mixed_in, ggate_in, gk_in), (mixed_out, ggate_out, gk_out)
    pairs = len(sources)
    own, cols, width = gin_hbm.shape

    def take(e):
        return pltpu.make_async_copy(held_hbm.at[:, e], held.at[e], in_sem.at[e])

    def give(e):
        return pltpu.make_async_copy(rows.at[e], gin_hbm.at[e], row_sem.at[e])

    factor = pltpu.make_async_copy(a_hbm, a, in_sem.at[own])
    factor.start()

    @pl.loop(0, own)
    def _(e):
        take(e).start()

    moves = []
    for i in range(pairs):
        size = sources[i].shape[0] // PIECES
        for p in range(PIECES):
            part = pl.ds(p * size, size)
            moves.append(
                pltpu.make_async_copy(
                    sources[i].at[part], targets[i].at[part], out_sem.at[i, p]
                )
            )
            moves[-1].start()
    factor.wait()

    @pl.loop(0, own)
    def _(e):
        take(e).wait()
        rows[e] = lax.dot_general(
            a[e],
            held[e].reshape(cols, width),
            (((0,), (0,)), ((), ())),
            preferred_element_type=jnp.float32,
        ).astype(rows.dtype)
        give(e).start()

    @pl.loop(0, own)
    def _(e):
        give(e).wait()

    for move in moves:
        move.wait()


def fused_shards(n, inputs, gate, kernel, first_blocks, second_blocks, cotangent):
    f32 = jnp.float32
    bf16 = jnp.bfloat16
    _, own, cols, width = inputs.shape
    rows = kernel.shape[0]
    slabs = width // LANES
    here = jax.ShapeDtypeStruct((own, cols, width), bf16)
    anywhere = pl.BlockSpec(memory_space=pl.ANY)
    wire = pltpu.VMEM((n, own, own, width), bf16)
    held = pltpu.VMEM((own, cols, width), bf16)
    dma = pltpu.SemaphoreType.DMA
    mixed, blocks, ggate, gk, _ = pl.pallas_call(
        functools.partial(fused, n),
        out_shape=(
            here,
            jax.ShapeDtypeStruct((n, own, own, width), bf16),
            here,
            jax.ShapeDtypeStruct((rows * own, width), f32),
            jax.ShapeDtypeStruct((own, rows, width), f32),
        ),
        in_specs=[anywhere] * 6,
        out_specs=[anywhere] * 5,
        scratch_shapes=[
            pltpu.VMEM((own, cols, cols), bf16),
            pltpu.VMEM((own, rows, rows), bf16),
            held,
            held,
            held,
            wire,
            wire,
            wire,
            wire,
            wire,
            pltpu.VMEM((own, rows, width), f32),
            pltpu.VMEM((slabs, cols // 2 * own, LANES), f32),
            pltpu.VMEM((rows // 4 * own, width), bf16),
            pltpu.VMEM((2, rows // 2, width), f32),
            dma((5,)),
            dma((2,)),
            dma((slabs,)),
            dma((4, n)),
            dma((4, n)),
            dma,
            dma,
        ],
        compiler_params=pltpu.CompilerParams(
            collective_id=0, has_side_effects=True, vmem_limit_bytes=60 << 20
        ),
        cost_estimate=pl.CostEstimate(
            flops=16 * own * cols * cols * width,
            bytes_accessed=48 * own * cols * width,
            transcendentals=0,
        ),
    )(
        inputs.reshape(own, cols, width),
        gate.reshape(own, cols, width),
        kernel.reshape(rows * own, width),
        first_blocks,
        second_blocks,
        cotangent.reshape(own, cols, width),
    )
    grads = jax.ShapeDtypeStruct((rows * own, width), f32)
    gin, mixed, ggate, gk = pl.pallas_call(
        last_rows,
        out_shape=(here, here, here, grads),
        in_specs=[anywhere] * 5,
        out_specs=[anywhere] * 4,
        scratch_shapes=[
            pltpu.VMEM((own, cols, cols), bf16),
            pltpu.VMEM((own, n, own, width), bf16),
            held,
            dma((own + 1,)),
            dma((own,)),
            dma((3, PIECES)),
        ],
        compiler_params=pltpu.CompilerParams(vmem_limit_bytes=60 << 20),
        cost_estimate=pl.CostEstimate(
            flops=2 * own * cols * cols * width,
            bytes_accessed=20 * own * cols * width,
            transcendentals=0,
        ),
    )(first_blocks, blocks, mixed, ggate, gk)
    shape = inputs.shape
    return (
        mixed.reshape(shape),
        gin.reshape(shape),
        ggate.reshape(shape),
        gk.reshape(rows, own, width),
    )


def shards(inputs, gate, kernel, first_blocks, second_blocks, cotangent):
    f32 = jnp.float32
    bf16 = jnp.bfloat16
    gate32 = gate.astype(f32)
    cot = cotangent.astype(f32)
    d_result = (cot * gate32).astype(bf16)

    def spread(rows):
        return jnp.einsum("rij,srjd->srid", first_blocks, rows, preferred_element_type=f32).astype(
            bf16
        )

    def mix_columns(piece):
        return jnp.einsum("cqr,srcd->sqcd", second_blocks, piece, preferred_element_type=f32)

    def unmix_columns(scaled):
        return jnp.einsum(
            "cqr,sqcd->srcd", second_blocks, scaled, preferred_element_type=f32
        ).astype(bf16)

    def finish_rows(piece):
        return jnp.einsum("rij,srid->srjd", first_blocks, piece, preferred_element_type=f32)

    second = mix_columns(
        lax.all_to_all(spread(inputs), "seq", split_axis=2, concat_axis=1, tiled=True)
    )
    hidden = (second * kernel).astype(bf16)
    result = finish_rows(
        lax.all_to_all(unmix_columns(hidden), "seq", split_axis=1, concat_axis=2, tiled=True)
    )
    d_hidden = mix_columns(
        lax.all_to_all(spread(d_result), "seq", split_axis=2, concat_axis=1, tiled=True)
    )
    d_second = (d_hidden * kernel).astype(bf16)
    d_inputs = finish_rows(
        lax.all_to_all(unmix_columns(d_second), "seq", split_axis=1, concat_axis=2, tiled=True)
    )
    mixed = (result * gate32).astype(bf16)
    grad_gate = (cot * result).astype(bf16)
    grad_inputs = d_inputs.astype(bf16)
    grad_kernel = lax.psum(jnp.sum(d_hidden * second, axis=0), "dp")
    return (mixed, grad_inputs, grad_gate, grad_kernel)


def solution(mesh):
    placed = (
        P("dp", "seq", None, None),
        P("dp", "seq", None, None),
        P(None, "seq", None),
        P("seq", None, None),
        P("seq", None, None),
        P("dp", "seq", None, None),
    )
    def program(inputs, gate, kernel, first_blocks, second_blocks, cotangent):
        n = mesh.shape["seq"]
        seqs, rows, cols, width = inputs.shape
        fits = (
            mesh.shape["dp"] == 2
            and seqs == 2
            and rows == cols
            and n % 2 == 0
            and rows % (16 * n) == 0
            and rows % 256 == 0
            and width % LANES == 0
        )
        body = functools.partial(fused_shards, n) if fits else shards
        return placed_body(body)(
            inputs, gate, kernel, first_blocks, second_blocks, cotangent
        )

    def placed_body(body):
        return jax.shard_map(
            body,
            mesh=mesh,
            in_specs=placed,
            out_specs=(
                P("dp", "seq", None, None),
                P("dp", "seq", None, None),
                P("dp", "seq", None, None),
                P(None, "seq", None),
            ),
            check_vma=False,
        )

    return program
```

```python
import functools

import jax
import jax.numpy as jnp
from jax import lax
from jax.experimental import pallas as pl
from jax.experimental.pallas import tpu as pltpu
from jax.sharding import PartitionSpec as P

MESH = pl.DeviceIdType.MESH
LANES = 128
PIECES = 4


def fused(
    n,
    x_hbm,
    gate_hbm,
    kern_hbm,
    a_hbm,
    b_hbm,
    cot_hbm,
    mixed_hbm,
    recv_2b,
    ggate_hbm,
    gk_hbm,
    part_hbm,
    a,
    b,
    x,
    gate,
    cot,
    send_f,
    send_b,
    recv_1f,
    recv_1b,
    recv_2f,
    second,
    turn,
    kst,
    tmp,
    load_sem,
    tmp_sem,
    out_sem,
    send_sem,
    recv_sem,
    dp_send,
    dp_recv,
):
    f32 = jnp.float32
    bf16 = jnp.bfloat16
    own, cols, width = x.shape
    rows = cols
    half = n // 2
    cut = cols // 2
    slabs = width // LANES
    block = own * own
    me = lax.axis_index("seq")
    other = 1 - lax.axis_index("dp")
    near_half = me // half
    far_half = 1 - near_half
    spot = me % half

    def load(src, dst, i):
        return pltpu.make_async_copy(src, dst, load_sem.at[i])

    load(a_hbm, a, 0).start()
    load(x_hbm, x, 1).start()
    load(gate_hbm, gate, 2).start()
    load(cot_hbm, cot, 3).start()
    load(b_hbm, b, 4).start()

    barrier = pltpu.get_barrier_semaphore()

    @pl.loop(1, n)
    def _(i):
        pl.semaphore_signal(
            barrier, inc=1, device_id={"seq": (me + i) % n}, device_id_type=MESH
        )

    pl.semaphore_signal(barrier, inc=1, device_id={"dp": other}, device_id_type=MESH)
    pl.semaphore_wait(barrier, n)

    def lane(k):
        return pl.ds(k * LANES, LANES)

    def message(stage, send, recv, to, slot):
        return pltpu.make_async_remote_copy(
            src_ref=send.at[to],
            dst_ref=recv.at[slot],
            send_sem=send_sem.at[stage, to],
            recv_sem=recv_sem.at[stage, slot],
            device_id={"seq": to},
            device_id_type=MESH,
        )

    def wait_sent(stage, send, recv):
        @pl.loop(1, n)
        def _(i):
            to = (me + i) % n
            message(stage, send, recv, to, to).wait_send()

    def wait_arrived(stage, send, recv):
        @pl.loop(1, n)
        def _(i):
            slot = (me + i) % n
            message(stage, send, recv, slot, slot).wait_recv()

    def produce(side, product, send):
        at = pl.multiple_of(side * cut, cut)

        @pl.loop(0, own)
        def _(e):
            value = product(e, at)
            for k in range(slabs):
                turn[k, pl.ds(e, cut, stride=own), :] = value[
                    :, k * LANES : (k + 1) * LANES
                ]

        @pl.loop(0, half)
        def _(j):
            for k in range(slabs):
                piece = turn[k, pl.ds(pl.multiple_of(j * block, block), block), :]
                send[side * half + j, :, :, k * LANES : (k + 1) * LANES] = piece.reshape(
                    own, own, LANES
                ).astype(bf16)

    def order(i):
        far = 1 - i % 2
        side = far * far_half + (1 - far) * near_half
        return side * half + (spot + (1 - far) + i // 2) % half

    def start(stage, send, recv, i):
        message(stage, send, recv, order(i), me).start()

    def exchange(stage, product, send, recv):
        produce(far_half, product, send)
        start(stage, send, recv, 0)
        start(stage, send, recv, 2)
        produce(near_half, product, send)
        start(stage, send, recv, 1)

        @pl.loop(3, n - 1)
        def _(i):
            start(stage, send, recv, i)

    def spread(e, at):
        return jnp.dot(a[e, pl.ds(at, cut), :], x[e], preferred_element_type=f32)

    def unmix(held):
        def product(e, at):
            values = held[:, e].reshape(rows, width)
            return lax.dot_general(
                b[e, :, pl.ds(at, cut)],
                values,
                (((0,), (0,)), ((), ())),
                preferred_element_type=f32,
            )

        return product

    def finish(held, e):
        return lax.dot_general(
            a[e],
            held[:, e].reshape(cols, width),
            (((0,), (0,)), ((), ())),
            preferred_element_type=f32,
        )

    load(a_hbm, a, 0).wait()
    load(x_hbm, x, 1).wait()
    exchange(0, spread, send_f, recv_1f)
    recv_1f[me] = send_f[me]

    load(gate_hbm, gate, 2).wait()
    load(cot_hbm, cot, 3).wait()

    @pl.loop(0, own)
    def _(e):
        x[e] = (cot[e].astype(f32) * gate[e].astype(f32)).astype(bf16)

    exchange(1, spread, send_b, recv_1b)
    recv_1b[me] = send_b[me]

    quarter = kst.shape[0] // own

    @pl.loop(0, rows // quarter)
    def _(i):
        size = quarter * own
        take = load(kern_hbm.at[pl.ds(pl.multiple_of(i * size, size), size), :], kst, 1)
        take.start()
        take.wait()
        for k in range(slabs):
            turn[k, 0:size, :] = kst[:, k * LANES : (k + 1) * LANES].astype(f32)

        @pl.loop(0, own)
        def _(e):
            for k in range(slabs):
                x[
                    e,
                    pl.ds(pl.multiple_of(i * quarter, quarter), quarter),
                    k * LANES : (k + 1) * LANES,
                ] = turn[k, pl.ds(e, quarter, stride=own), :].astype(bf16)

    load(b_hbm, b, 4).wait()
    wait_arrived(0, send_f, recv_1f)

    @pl.loop(0, own)
    def _(e):
        value = jnp.dot(
            b[e], recv_1f[:, e].reshape(rows, width), preferred_element_type=f32
        )
        second[e] = value
        recv_1f[:, e] = (value * x[e].astype(f32)).astype(bf16).reshape(n, own, width)

    wait_sent(0, send_f, recv_1f)
    exchange(2, unmix(recv_1f), send_f, recv_2f)

    recv_2f[me] = send_f[me]

    wait_arrived(1, send_b, recv_1b)

    @pl.loop(0, own)
    def _(e):
        value = jnp.dot(
            b[e], recv_1b[:, e].reshape(rows, width), preferred_element_type=f32
        )
        second[e] = second[e] * value
        recv_1b[:, e] = (value * x[e].astype(f32)).astype(bf16).reshape(n, own, width)

    swap = pltpu.make_async_remote_copy(
        src_ref=second,
        dst_ref=part_hbm,
        send_sem=dp_send,
        recv_sem=dp_recv,
        device_id={"dp": other},
        device_id_type=MESH,
    )
    swap.start()
    wait_sent(1, send_b, recv_1b)
    exchange(3, unmix(recv_1b), send_b, recv_2b)
    keep = load(send_b.at[me], recv_2b.at[me], 0)
    keep.start()

    swap.wait_recv()
    for side in range(2):
        at = side * cut

        def part(e, slot):
            return pltpu.make_async_copy(
                part_hbm.at[e, pl.ds(at, cut), :], tmp.at[slot], tmp_sem.at[slot]
            )

        part(0, 0).start()

        @pl.loop(0, own)
        def _(e):
            @pl.when(e < own - 1)
            def _():
                part(e + 1, (e + 1) % 2).start()

            part(e, e % 2).wait()
            total = second[e, at : at + cut, :] + tmp[e % 2]
            for k in range(slabs):
                turn[k, pl.ds(e, cut, stride=own), :] = total[
                    :, k * LANES : (k + 1) * LANES
                ]

        outs = [
            pltpu.make_async_copy(
                turn.at[k],
                gk_hbm.at[pl.ds(at * own, cut * own), lane(k)],
                out_sem.at[k],
            )
            for k in range(slabs)
        ]
        for out in outs:
            out.start()
        for out in outs:
            out.wait()

    wait_arrived(2, send_f, recv_2f)

    @pl.loop(0, own)
    def _(e):
        result = finish(recv_2f, e)
        mixed = (result * gate[e].astype(f32)).astype(bf16)
        ggate = (cot[e].astype(f32) * result).astype(bf16)
        gate[e] = mixed
        cot[e] = ggate

    out_mixed = load(gate, mixed_hbm, 2)
    out_ggate = load(cot, ggate_hbm, 3)
    out_mixed.start()
    out_ggate.start()

    swap.wait_send()
    wait_arrived(3, send_b, recv_2b)

    wait_sent(2, send_f, recv_2f)
    wait_sent(3, send_b, recv_2b)
    keep.wait()
    out_mixed.wait()
    out_ggate.wait()


def last_rows(
    a_hbm,
    held_hbm,
    mixed_in,
    ggate_in,
    gk_in,
    gin_hbm,
    mixed_out,
    ggate_out,
    gk_out,
    a,
    held,
    rows,
    mixed,
    ggate,
    gk,
    in_sem,
    row_sem,
    pass_sem,
    out_sem,
):
    own, cols, width = gin_hbm.shape

    def take(e):
        return pltpu.make_async_copy(held_hbm.at[:, e], held.at[e], in_sem.at[e])

    def give(e):
        return pltpu.make_async_copy(rows.at[e], gin_hbm.at[e], row_sem.at[e])

    def through(i, source, stage, target):
        size = source.shape[0] // PIECES
        moves = []
        for p in range(PIECES):
            part = pl.ds(p * size, size)
            moves.append(
                (
                    pltpu.make_async_copy(
                        source.at[part], stage.at[part], pass_sem.at[i, p]
                    ),
                    pltpu.make_async_copy(
                        stage.at[part], target.at[part], out_sem.at[i, p]
                    ),
                )
            )
        return moves

    moves = (
        through(0, mixed_in, mixed, mixed_out)
        + through(1, ggate_in, ggate, ggate_out)
        + through(2, gk_in, gk, gk_out)
    )
    factor = pltpu.make_async_copy(a_hbm, a, in_sem.at[own])
    factor.start()
    for e in range(max(own, len(moves))):
        if e < len(moves):
            moves[e][0].start()
        if e < own:
            take(e).start()
    factor.wait()
    for e in range(max(own, len(moves))):
        if e < len(moves):
            moves[e][0].wait()
            moves[e][1].start()
        if e < own:
            take(e).wait()
            rows[e] = lax.dot_general(
                a[e],
                held[e].reshape(cols, width),
                (((0,), (0,)), ((), ())),
                preferred_element_type=jnp.float32,
            ).astype(rows.dtype)
            give(e).start()
    for e in range(own):
        give(e).wait()
    for move in moves:
        move[1].wait()


def fused_shards(n, inputs, gate, kernel, first_blocks, second_blocks, cotangent):
    f32 = jnp.float32
    bf16 = jnp.bfloat16
    _, own, cols, width = inputs.shape
    rows = kernel.shape[0]
    slabs = width // LANES
    here = jax.ShapeDtypeStruct((own, cols, width), bf16)
    anywhere = pl.BlockSpec(memory_space=pl.ANY)
    wire = pltpu.VMEM((n, own, own, width), bf16)
    held = pltpu.VMEM((own, cols, width), bf16)
    dma = pltpu.SemaphoreType.DMA
    mixed, blocks, ggate, gk, _ = pl.pallas_call(
        functools.partial(fused, n),
        out_shape=(
            here,
            jax.ShapeDtypeStruct((n, own, own, width), bf16),
            here,
            jax.ShapeDtypeStruct((rows * own, width), f32),
            jax.ShapeDtypeStruct((own, rows, width), f32),
        ),
        in_specs=[anywhere] * 6,
        out_specs=[anywhere] * 5,
        scratch_shapes=[
            pltpu.VMEM((own, cols, cols), bf16),
            pltpu.VMEM((own, rows, rows), bf16),
            held,
            held,
            held,
            wire,
            wire,
            wire,
            wire,
            wire,
            pltpu.VMEM((own, rows, width), f32),
            pltpu.VMEM((slabs, cols // 2 * own, LANES), f32),
            pltpu.VMEM((rows // 4 * own, width), bf16),
            pltpu.VMEM((2, rows // 2, width), f32),
            dma((5,)),
            dma((2,)),
            dma((slabs,)),
            dma((4, n)),
            dma((4, n)),
            dma,
            dma,
        ],
        compiler_params=pltpu.CompilerParams(
            collective_id=0, has_side_effects=True, vmem_limit_bytes=60 << 20
        ),
        cost_estimate=pl.CostEstimate(
            flops=16 * own * cols * cols * width,
            bytes_accessed=48 * own * cols * width,
            transcendentals=0,
        ),
    )(
        inputs.reshape(own, cols, width),
        gate.reshape(own, cols, width),
        kernel.reshape(rows * own, width),
        first_blocks,
        second_blocks,
        cotangent.reshape(own, cols, width),
    )
    grads = jax.ShapeDtypeStruct((rows * own, width), f32)
    gin, mixed, ggate, gk = pl.pallas_call(
        last_rows,
        out_shape=(here, here, here, grads),
        in_specs=[anywhere] * 5,
        out_specs=[anywhere] * 4,
        scratch_shapes=[
            pltpu.VMEM((own, cols, cols), bf16),
            pltpu.VMEM((own, n, own, width), bf16),
            held,
            held,
            held,
            pltpu.VMEM((rows * own, width), f32),
            dma((own + 1,)),
            dma((own,)),
            dma((3, PIECES)),
            dma((3, PIECES)),
        ],
        compiler_params=pltpu.CompilerParams(vmem_limit_bytes=60 << 20),
        cost_estimate=pl.CostEstimate(
            flops=2 * own * cols * cols * width,
            bytes_accessed=20 * own * cols * width,
            transcendentals=0,
        ),
    )(first_blocks, blocks, mixed, ggate, gk)
    shape = inputs.shape
    return (
        mixed.reshape(shape),
        gin.reshape(shape),
        ggate.reshape(shape),
        gk.reshape(rows, own, width),
    )


def shards(inputs, gate, kernel, first_blocks, second_blocks, cotangent):
    f32 = jnp.float32
    bf16 = jnp.bfloat16
    gate32 = gate.astype(f32)
    cot = cotangent.astype(f32)
    d_result = (cot * gate32).astype(bf16)

    def spread(rows):
        return jnp.einsum("rij,srjd->srid", first_blocks, rows, preferred_element_type=f32).astype(
            bf16
        )

    def mix_columns(piece):
        return jnp.einsum("cqr,srcd->sqcd", second_blocks, piece, preferred_element_type=f32)

    def unmix_columns(scaled):
        return jnp.einsum(
            "cqr,sqcd->srcd", second_blocks, scaled, preferred_element_type=f32
        ).astype(bf16)

    def finish_rows(piece):
        return jnp.einsum("rij,srid->srjd", first_blocks, piece, preferred_element_type=f32)

    second = mix_columns(
        lax.all_to_all(spread(inputs), "seq", split_axis=2, concat_axis=1, tiled=True)
    )
    hidden = (second * kernel).astype(bf16)
    result = finish_rows(
        lax.all_to_all(unmix_columns(hidden), "seq", split_axis=1, concat_axis=2, tiled=True)
    )
    d_hidden = mix_columns(
        lax.all_to_all(spread(d_result), "seq", split_axis=2, concat_axis=1, tiled=True)
    )
    d_second = (d_hidden * kernel).astype(bf16)
    d_inputs = finish_rows(
        lax.all_to_all(unmix_columns(d_second), "seq", split_axis=1, concat_axis=2, tiled=True)
    )
    mixed = (result * gate32).astype(bf16)
    grad_gate = (cot * result).astype(bf16)
    grad_inputs = d_inputs.astype(bf16)
    grad_kernel = lax.psum(jnp.sum(d_hidden * second, axis=0), "dp")
    return (mixed, grad_inputs, grad_gate, grad_kernel)


def solution(mesh):
    placed = (
        P("dp", "seq", None, None),
        P("dp", "seq", None, None),
        P(None, "seq", None),
        P("seq", None, None),
        P("seq", None, None),
        P("dp", "seq", None, None),
    )
    def program(inputs, gate, kernel, first_blocks, second_blocks, cotangent):
        n = mesh.shape["seq"]
        seqs, rows, cols, width = inputs.shape
        fits = (
            mesh.shape["dp"] == 2
            and seqs == 2
            and rows == cols
            and n % 2 == 0
            and rows % (16 * n) == 0
            and rows % 256 == 0
            and width % LANES == 0
        )
        body = functools.partial(fused_shards, n) if fits else shards
        return placed_body(body)(
            inputs, gate, kernel, first_blocks, second_blocks, cotangent
        )

    def placed_body(body):
        return jax.shard_map(
            body,
            mesh=mesh,
            in_specs=placed,
            out_specs=(
                P("dp", "seq", None, None),
                P("dp", "seq", None, None),
                P("dp", "seq", None, None),
                P(None, "seq", None),
            ),
            check_vma=False,
        )

    return program
```

```python
import functools

import jax
import jax.numpy as jnp
from jax import lax
from jax.experimental import pallas as pl
from jax.experimental.pallas import tpu as pltpu
from jax.sharding import PartitionSpec as P

MESH = pl.DeviceIdType.MESH
LANES = 128
PIECES = 4


def fused(
    n,
    x_hbm,
    gate_hbm,
    kern_hbm,
    a_hbm,
    b_hbm,
    cot_hbm,
    mixed_hbm,
    recv_2b,
    ggate_hbm,
    gk_hbm,
    part_hbm,
    a,
    b,
    x,
    gate,
    cot,
    send_f,
    send_b,
    recv_1f,
    recv_1b,
    recv_2f,
    second,
    turn,
    kst,
    tmp,
    load_sem,
    tmp_sem,
    out_sem,
    send_sem,
    recv_sem,
    dp_send,
    dp_recv,
):
    f32 = jnp.float32
    bf16 = jnp.bfloat16
    own, cols, width = x.shape
    rows = cols
    half = n // 2
    cut = cols // 2
    slabs = width // LANES
    block = own * own
    me = lax.axis_index("seq")
    other = 1 - lax.axis_index("dp")
    near_half = me // half
    far_half = 1 - near_half
    spot = me % half

    def load(src, dst, i):
        return pltpu.make_async_copy(src, dst, load_sem.at[i])

    load(a_hbm, a, 0).start()
    load(x_hbm, x, 1).start()

    barrier = pltpu.get_barrier_semaphore()

    @pl.loop(1, n)
    def _(i):
        pl.semaphore_signal(
            barrier, inc=1, device_id={"seq": (me + i) % n}, device_id_type=MESH
        )

    pl.semaphore_signal(barrier, inc=1, device_id={"dp": other}, device_id_type=MESH)
    pl.semaphore_wait(barrier, n)

    def lane(k):
        return pl.ds(k * LANES, LANES)

    def message(stage, send, recv, to, slot):
        return pltpu.make_async_remote_copy(
            src_ref=send.at[to],
            dst_ref=recv.at[slot],
            send_sem=send_sem.at[stage, to],
            recv_sem=recv_sem.at[stage, slot],
            device_id={"seq": to},
            device_id_type=MESH,
        )

    def wait_sent(stage, send, recv):
        @pl.loop(1, n)
        def _(i):
            to = (me + i) % n
            message(stage, send, recv, to, to).wait_send()

    def wait_arrived(stage, send, recv):
        @pl.loop(1, n)
        def _(i):
            slot = (me + i) % n
            message(stage, send, recv, slot, slot).wait_recv()

    def produce(side, product, send):
        at = pl.multiple_of(side * cut, cut)

        @pl.loop(0, own)
        def _(e):
            value = product(e, at)
            for k in range(slabs):
                turn[k, pl.ds(e, cut, stride=own), :] = value[
                    :, k * LANES : (k + 1) * LANES
                ]

        @pl.loop(0, half)
        def _(j):
            for k in range(slabs):
                piece = turn[k, pl.ds(pl.multiple_of(j * block, block), block), :]
                send[side * half + j, :, :, k * LANES : (k + 1) * LANES] = piece.reshape(
                    own, own, LANES
                ).astype(bf16)

    def order(i):
        far = 1 - i % 2
        side = far * far_half + (1 - far) * near_half
        return side * half + (spot + (1 - far) + i // 2) % half

    def start(stage, send, recv, i):
        message(stage, send, recv, order(i), me).start()

    def exchange(stage, product, send, recv):
        produce(far_half, product, send)
        start(stage, send, recv, 0)
        start(stage, send, recv, 2)
        produce(near_half, product, send)
        start(stage, send, recv, 1)

        @pl.loop(3, n - 1)
        def _(i):
            start(stage, send, recv, i)

    def spread(e, at):
        return jnp.dot(a[e, pl.ds(at, cut), :], x[e], preferred_element_type=f32)

    def unmix(held):
        def product(e, at):
            values = held[:, e].reshape(rows, width)
            return lax.dot_general(
                b[e, :, pl.ds(at, cut)],
                values,
                (((0,), (0,)), ((), ())),
                preferred_element_type=f32,
            )

        return product

    def finish(held, e):
        return lax.dot_general(
            a[e],
            held[:, e].reshape(cols, width),
            (((0,), (0,)), ((), ())),
            preferred_element_type=f32,
        )

    load(a_hbm, a, 0).wait()
    load(x_hbm, x, 1).wait()
    load(gate_hbm, gate, 2).start()
    load(cot_hbm, cot, 3).start()
    load(b_hbm, b, 4).start()
    exchange(0, spread, send_f, recv_1f)
    recv_1f[me] = send_f[me]

    load(gate_hbm, gate, 2).wait()
    load(cot_hbm, cot, 3).wait()

    @pl.loop(0, own)
    def _(e):
        x[e] = (cot[e].astype(f32) * gate[e].astype(f32)).astype(bf16)

    exchange(1, spread, send_b, recv_1b)
    recv_1b[me] = send_b[me]

    quarter = kst.shape[0] // own

    @pl.loop(0, rows // quarter)
    def _(i):
        size = quarter * own
        take = load(kern_hbm.at[pl.ds(pl.multiple_of(i * size, size), size), :], kst, 1)
        take.start()
        take.wait()
        for k in range(slabs):
            turn[k, 0:size, :] = kst[:, k * LANES : (k + 1) * LANES].astype(f32)

        @pl.loop(0, own)
        def _(e):
            for k in range(slabs):
                x[
                    e,
                    pl.ds(pl.multiple_of(i * quarter, quarter), quarter),
                    k * LANES : (k + 1) * LANES,
                ] = turn[k, pl.ds(e, quarter, stride=own), :].astype(bf16)

    load(b_hbm, b, 4).wait()
    wait_arrived(0, send_f, recv_1f)

    @pl.loop(0, own)
    def _(e):
        value = jnp.dot(
            b[e], recv_1f[:, e].reshape(rows, width), preferred_element_type=f32
        )
        second[e] = value
        recv_1f[:, e] = (value * x[e].astype(f32)).astype(bf16).reshape(n, own, width)

    wait_sent(0, send_f, recv_1f)
    exchange(2, unmix(recv_1f), send_f, recv_2f)

    recv_2f[me] = send_f[me]

    wait_arrived(1, send_b, recv_1b)

    @pl.loop(0, own)
    def _(e):
        value = jnp.dot(
            b[e], recv_1b[:, e].reshape(rows, width), preferred_element_type=f32
        )
        second[e] = second[e] * value
        recv_1b[:, e] = (value * x[e].astype(f32)).astype(bf16).reshape(n, own, width)

    swap = pltpu.make_async_remote_copy(
        src_ref=second,
        dst_ref=part_hbm,
        send_sem=dp_send,
        recv_sem=dp_recv,
        device_id={"dp": other},
        device_id_type=MESH,
    )
    swap.start()
    wait_sent(1, send_b, recv_1b)
    exchange(3, unmix(recv_1b), send_b, recv_2b)
    keep = load(send_b.at[me], recv_2b.at[me], 0)
    keep.start()

    swap.wait_recv()
    for side in range(2):
        at = side * cut

        def part(e, slot):
            return pltpu.make_async_copy(
                part_hbm.at[e, pl.ds(at, cut), :], tmp.at[slot], tmp_sem.at[slot]
            )

        part(0, 0).start()

        @pl.loop(0, own)
        def _(e):
            @pl.when(e < own - 1)
            def _():
                part(e + 1, (e + 1) % 2).start()

            part(e, e % 2).wait()
            total = second[e, at : at + cut, :] + tmp[e % 2]
            for k in range(slabs):
                turn[k, pl.ds(e, cut, stride=own), :] = total[
                    :, k * LANES : (k + 1) * LANES
                ]

        outs = [
            pltpu.make_async_copy(
                turn.at[k],
                gk_hbm.at[pl.ds(at * own, cut * own), lane(k)],
                out_sem.at[k],
            )
            for k in range(slabs)
        ]
        for out in outs:
            out.start()
        for out in outs:
            out.wait()

    wait_arrived(2, send_f, recv_2f)

    @pl.loop(0, own)
    def _(e):
        result = finish(recv_2f, e)
        mixed = (result * gate[e].astype(f32)).astype(bf16)
        ggate = (cot[e].astype(f32) * result).astype(bf16)
        gate[e] = mixed
        cot[e] = ggate

    out_mixed = load(gate, mixed_hbm, 2)
    out_ggate = load(cot, ggate_hbm, 3)
    out_mixed.start()
    out_ggate.start()

    swap.wait_send()
    wait_arrived(3, send_b, recv_2b)

    wait_sent(2, send_f, recv_2f)
    wait_sent(3, send_b, recv_2b)
    keep.wait()
    out_mixed.wait()
    out_ggate.wait()


def last_rows(
    a_hbm,
    held_hbm,
    mixed_in,
    ggate_in,
    gk_in,
    gin_hbm,
    mixed_out,
    ggate_out,
    gk_out,
    a,
    held,
    rows,
    mixed,
    ggate,
    gk,
    in_sem,
    row_sem,
    pass_sem,
    out_sem,
):
    own, cols, width = gin_hbm.shape

    def take(e):
        return pltpu.make_async_copy(held_hbm.at[:, e], held.at[e], in_sem.at[e])

    def give(e):
        return pltpu.make_async_copy(rows.at[e], gin_hbm.at[e], row_sem.at[e])

    def through(i, source, stage, target):
        size = source.shape[0] // PIECES
        moves = []
        for p in range(PIECES):
            part = pl.ds(p * size, size)
            moves.append(
                (
                    pltpu.make_async_copy(
                        source.at[part], stage.at[part], pass_sem.at[i, p]
                    ),
                    pltpu.make_async_copy(
                        stage.at[part], target.at[part], out_sem.at[i, p]
                    ),
                )
            )
        return moves

    moves = (
        through(0, mixed_in, mixed, mixed_out)
        + through(1, ggate_in, ggate, ggate_out)
        + through(2, gk_in, gk, gk_out)
    )
    factor = pltpu.make_async_copy(a_hbm, a, in_sem.at[own])
    factor.start()
    for e in range(max(own, len(moves))):
        if e < len(moves):
            moves[e][0].start()
        if e < own:
            take(e).start()
    factor.wait()
    for e in range(max(own, len(moves))):
        if e < len(moves):
            moves[e][0].wait()
            moves[e][1].start()
        if e < own:
            take(e).wait()
            rows[e] = lax.dot_general(
                a[e],
                held[e].reshape(cols, width),
                (((0,), (0,)), ((), ())),
                preferred_element_type=jnp.float32,
            ).astype(rows.dtype)
            give(e).start()
    for e in range(own):
        give(e).wait()
    for move in moves:
        move[1].wait()


def fused_shards(n, inputs, gate, kernel, first_blocks, second_blocks, cotangent):
    f32 = jnp.float32
    bf16 = jnp.bfloat16
    _, own, cols, width = inputs.shape
    rows = kernel.shape[0]
    slabs = width // LANES
    here = jax.ShapeDtypeStruct((own, cols, width), bf16)
    anywhere = pl.BlockSpec(memory_space=pl.ANY)
    wire = pltpu.VMEM((n, own, own, width), bf16)
    held = pltpu.VMEM((own, cols, width), bf16)
    dma = pltpu.SemaphoreType.DMA
    mixed, blocks, ggate, gk, _ = pl.pallas_call(
        functools.partial(fused, n),
        out_shape=(
            here,
            jax.ShapeDtypeStruct((n, own, own, width), bf16),
            here,
            jax.ShapeDtypeStruct((rows * own, width), f32),
            jax.ShapeDtypeStruct((own, rows, width), f32),
        ),
        in_specs=[anywhere] * 6,
        out_specs=[anywhere] * 5,
        scratch_shapes=[
            pltpu.VMEM((own, cols, cols), bf16),
            pltpu.VMEM((own, rows, rows), bf16),
            held,
            held,
            held,
            wire,
            wire,
            wire,
            wire,
            wire,
            pltpu.VMEM((own, rows, width), f32),
            pltpu.VMEM((slabs, cols // 2 * own, LANES), f32),
            pltpu.VMEM((rows // 4 * own, width), bf16),
            pltpu.VMEM((2, rows // 2, width), f32),
            dma((5,)),
            dma((2,)),
            dma((slabs,)),
            dma((4, n)),
            dma((4, n)),
            dma,
            dma,
        ],
        compiler_params=pltpu.CompilerParams(
            collective_id=0, has_side_effects=True, vmem_limit_bytes=60 << 20
        ),
        cost_estimate=pl.CostEstimate(
            flops=16 * own * cols * cols * width,
            bytes_accessed=48 * own * cols * width,
            transcendentals=0,
        ),
    )(
        inputs.reshape(own, cols, width),
        gate.reshape(own, cols, width),
        kernel.reshape(rows * own, width),
        first_blocks,
        second_blocks,
        cotangent.reshape(own, cols, width),
    )
    grads = jax.ShapeDtypeStruct((rows * own, width), f32)
    gin, mixed, ggate, gk = pl.pallas_call(
        last_rows,
        out_shape=(here, here, here, grads),
        in_specs=[anywhere] * 5,
        out_specs=[anywhere] * 4,
        scratch_shapes=[
            pltpu.VMEM((own, cols, cols), bf16),
            pltpu.VMEM((own, n, own, width), bf16),
            held,
            held,
            held,
            pltpu.VMEM((rows * own, width), f32),
            dma((own + 1,)),
            dma((own,)),
            dma((3, PIECES)),
            dma((3, PIECES)),
        ],
        compiler_params=pltpu.CompilerParams(vmem_limit_bytes=60 << 20),
        cost_estimate=pl.CostEstimate(
            flops=2 * own * cols * cols * width,
            bytes_accessed=20 * own * cols * width,
            transcendentals=0,
        ),
    )(first_blocks, blocks, mixed, ggate, gk)
    shape = inputs.shape
    return (
        mixed.reshape(shape),
        gin.reshape(shape),
        ggate.reshape(shape),
        gk.reshape(rows, own, width),
    )


def shards(inputs, gate, kernel, first_blocks, second_blocks, cotangent):
    f32 = jnp.float32
    bf16 = jnp.bfloat16
    gate32 = gate.astype(f32)
    cot = cotangent.astype(f32)
    d_result = (cot * gate32).astype(bf16)

    def spread(rows):
        return jnp.einsum("rij,srjd->srid", first_blocks, rows, preferred_element_type=f32).astype(
            bf16
        )

    def mix_columns(piece):
        return jnp.einsum("cqr,srcd->sqcd", second_blocks, piece, preferred_element_type=f32)

    def unmix_columns(scaled):
        return jnp.einsum(
            "cqr,sqcd->srcd", second_blocks, scaled, preferred_element_type=f32
        ).astype(bf16)

    def finish_rows(piece):
        return jnp.einsum("rij,srid->srjd", first_blocks, piece, preferred_element_type=f32)

    second = mix_columns(
        lax.all_to_all(spread(inputs), "seq", split_axis=2, concat_axis=1, tiled=True)
    )
    hidden = (second * kernel).astype(bf16)
    result = finish_rows(
        lax.all_to_all(unmix_columns(hidden), "seq", split_axis=1, concat_axis=2, tiled=True)
    )
    d_hidden = mix_columns(
        lax.all_to_all(spread(d_result), "seq", split_axis=2, concat_axis=1, tiled=True)
    )
    d_second = (d_hidden * kernel).astype(bf16)
    d_inputs = finish_rows(
        lax.all_to_all(unmix_columns(d_second), "seq", split_axis=1, concat_axis=2, tiled=True)
    )
    mixed = (result * gate32).astype(bf16)
    grad_gate = (cot * result).astype(bf16)
    grad_inputs = d_inputs.astype(bf16)
    grad_kernel = lax.psum(jnp.sum(d_hidden * second, axis=0), "dp")
    return (mixed, grad_inputs, grad_gate, grad_kernel)


def solution(mesh):
    placed = (
        P("dp", "seq", None, None),
        P("dp", "seq", None, None),
        P(None, "seq", None),
        P("seq", None, None),
        P("seq", None, None),
        P("dp", "seq", None, None),
    )
    def program(inputs, gate, kernel, first_blocks, second_blocks, cotangent):
        n = mesh.shape["seq"]
        seqs, rows, cols, width = inputs.shape
        fits = (
            mesh.shape["dp"] == 2
            and seqs == 2
            and rows == cols
            and n % 2 == 0
            and rows % (16 * n) == 0
            and rows % 256 == 0
            and width % LANES == 0
        )
        body = functools.partial(fused_shards, n) if fits else shards
        return placed_body(body)(
            inputs, gate, kernel, first_blocks, second_blocks, cotangent
        )

    def placed_body(body):
        return jax.shard_map(
            body,
            mesh=mesh,
            in_specs=placed,
            out_specs=(
                P("dp", "seq", None, None),
                P("dp", "seq", None, None),
                P("dp", "seq", None, None),
                P(None, "seq", None),
            ),
            check_vma=False,
        )

    return program
```
